256 devices in a mesh: blk: 16 (over z, y_hi), tp: 16 (over x, y_lo, core).
Axes of the slice: x: 4, y: 4 (y_hi: 2, y_lo: 2; y = y_hi * 2 + y_lo), z: 8, core: 2. Of those that a mesh axis runs over, the one named last changes fastest.
Arguments:
- gate_pre: bfloat16 [8192, 13824], P('blk', 'tp'), may hold values from -6 to 6
- up_pre: bfloat16 [8192, 13824], P('blk', 'tp'), may hold values from -6 to 6
- down_weight: bfloat16 [5120, 13824], P('blk', 'tp'), may hold values from -0.0546875 to 0.0546875
- d_mixed: bfloat16 [8192, 5120], P('blk', 'tp'), may hold values from -6 to 6
Outputs:
- mixed: bfloat16 [8192, 5120], P('blk', 'tp')
- d_gate: bfloat16 [8192, 13824], P('blk', 'tp')
- d_up: bfloat16 [8192, 13824], P('blk', 'tp')
- grad_down: float32 [5120, 13824], P('blk', 'tp')
The draws below stay inside these ranges and needn't reach their ends.
All inputs are finite; a program needn't handle non-finite values.
Results may differ from the reference program's by a relative error of at most 0.022.
Values may be sent and summed in bfloat16 or wider, within the bound.
No kernel may reach another device: no remote copies, remote signals or barrier semaphores. Data moves between devices by JAX's collectives and lax.ppermute only.
A program may use at most 128 MiB of HBM per device.

```python
import jax
import jax.numpy as jnp
from jax import lax

D = 5120
FF = 13824
TOK_DEV = 512
TOKENS = 8192
N_BLK = 16
N_TP = 16


def strengthened(values, stream_key, source, target, parts, factor):
    def block_of(position):
        return (jnp.arange(values.shape[position]) // (values.shape[position] // parts)).reshape((-1,) + (1,) * (values.ndim - 1 - position))

    first = jax.random.permutation(stream_key, parts)[block_of(target)]
    other_side = (block_of(target) + parts // 2) % parts
    return jnp.where((block_of(source) == first) | (block_of(source) == other_side), factor * values, values)


def levels(own_key, extent, pieces, least, largest):
    factor_of, own = 1.0, jax.random.fold_in(own_key, 6)
    for dim, shards_of in pieces:
        steps = jnp.exp(jax.random.uniform(jax.random.fold_in(own, dim), (shards_of,), jnp.float32, least / len(pieces), largest / len(pieces)))
        factor_of = factor_of * jnp.repeat(steps, extent[dim] // shards_of).reshape([-1 if axis == dim else 1 for axis in range(len(extent))])
    return factor_of


def noise(own_key, shape, deviation, reach, pieces=(), kind=jnp.bfloat16):
    array = jax.random.normal(own_key, shape, jnp.float32) * deviation
    if len(pieces) > 0:
        array = levels(own_key, shape, pieces, -0.22, 0.18) * array
    return jnp.clip(array, min=-reach, max=reach).astype(kind)


def noise_with(rng, extent, deviation, most, cuts, heavy, kind=jnp.bfloat16):
    values = deviation * jax.random.normal(rng, extent, jnp.float32)
    if cuts:
        values = values * levels(rng, extent, cuts, -0.22, 0.18)
    return jnp.clip(strengthened(values, jax.random.fold_in(rng, 3), *heavy), -most, most).astype(kind)


def setup_inputs(seed: int = 0) -> dict:
    splits = jax.random.split(jax.random.key(seed), 5)
    return {
        "gate_pre": noise(splits[0], (TOKENS, FF), 1.0, 6.0, ((0, 16), (1, 16))),
        "up_pre": noise(splits[1], (TOKENS, FF), 1.0, 6.0, ((0, 16), (1, 16))),
        "down_weight": noise(splits[2], (D, FF), FF ** -0.5, 0.0546875, ((0, 16), (1, 16))),
        "d_mixed": noise_with(splits[3], (TOKENS, D), 1.0, 6.0, ((0, 16), (1, 16)), (0, 1, 16, 2.0)),
    }


def reference(gate_pre, up_pre, down_weight, d_mixed):
    gate_value = gate_pre.astype(jnp.float32)
    up_value = up_pre.astype(jnp.float32)
    sigmoid_gate = jax.nn.sigmoid(gate_value)
    activated = gate_value * sigmoid_gate
    hidden = (activated * up_value).astype(jnp.bfloat16)
    width_block = FF // N_TP

    def add_block(total, index):
        start = (index * width_block).astype(jnp.int32)
        hidden_part = lax.dynamic_slice_in_dim(hidden, start, width_block, 1)
        weight_part = lax.dynamic_slice_in_dim(down_weight, start, width_block, 1)
        partial_value = lax.dot_general(hidden_part, weight_part, (((1,), (1,)), ((), ())), preferred_element_type=jnp.float32)
        return total + partial_value.astype(jnp.bfloat16).astype(jnp.float32), None

    summed, _ = lax.scan(add_block, jnp.zeros((TOKENS, D), jnp.float32), jnp.arange(N_TP, dtype=jnp.int32))
    mixed = summed.astype(jnp.bfloat16)
    d_hidden = jnp.dot(d_mixed, down_weight, preferred_element_type=jnp.float32)
    d_gate = (d_hidden * up_value * sigmoid_gate * (1.0 + gate_value * (1.0 - sigmoid_gate))).astype(jnp.bfloat16)
    d_up = (d_hidden * activated).astype(jnp.bfloat16)

    def add_batch(total, index):
        start = (index * TOK_DEV).astype(jnp.int32)
        cot_rows = lax.dynamic_slice_in_dim(d_mixed, start, TOK_DEV, 0)
        hidden_rows = lax.dynamic_slice_in_dim(hidden, start, TOK_DEV, 0)
        term = lax.dot_general(cot_rows, hidden_rows, (((0,), (0,)), ((), ())), preferred_element_type=jnp.float32)
        return total + term.astype(jnp.bfloat16).astype(jnp.float32), None

    grad_down, _ = lax.scan(add_batch, jnp.zeros((D, FF), jnp.float32), jnp.arange(N_BLK, dtype=jnp.int32))
    return (mixed, d_gate, d_up, grad_down)
```

```python
import jax
import jax.numpy as jnp
from jax import lax
from jax.sharding import PartitionSpec as P

AXES = ("blk", "tp")
PLANES = [[2 * z + half for z in range(8)] for half in range(2)]


def route(move):
    pairs = []
    for x in range(4):
        for hi in range(2):
            for lo in range(2):
                for z in range(8):
                    for core in range(2):
                        tx, thi, tlo, tz, tcore = move(x, hi, lo, z, core)
                        source = (z * 2 + hi) * 16 + x * 4 + lo * 2 + core
                        target = (tz * 2 + thi) * 16 + (tx % 4) * 4 + tlo * 2 + tcore
                        pairs.append((source, target))
    return pairs


SIBLING = route(lambda x, hi, lo, z, c: (x, hi, lo, z, 1 - c))
PARTNER = route(lambda x, hi, lo, z, c: (x, 1 - hi, lo, z, c))
TURN = route(lambda x, hi, lo, z, c: (x, c, lo, z, hi))
TURN_LO = route(lambda x, hi, lo, z, c: (x, c, 1 - lo, z, hi))
ALONG_X = {d: route(lambda x, hi, lo, z, c, d=d: (x + d, hi, lo, z, c)) for d in (1, 2, 3)}


def send(value, pairs):
    return lax.ppermute(value, AXES, pairs)


def f32(value):
    return value.astype(jnp.float32)


def bf16(value):
    return value.astype(jnp.bfloat16)


def dot(left, right, dims):
    return lax.dot_general(left, right, ((dims[0], dims[1]), ((), ())), preferred_element_type=jnp.float32)


def first(value, *after):
    return lax.optimization_barrier((value, *after))[0]


def body(gate_pre, up_pre, down_weight, d_mixed):
    blk, tp = lax.axis_index("blk").astype(jnp.uint32), lax.axis_index("tp").astype(jnp.uint32)
    hi, core, lo, x = blk & 1, tp & 1, (tp >> 1) & 1, tp >> 2
    same = hi == core
    zero = jnp.uint32(0)

    def rows(step):
        return ((x + step) & 3) * 640

    weight = lax.all_gather(down_weight, "blk", axis_index_groups=PLANES, axis=0, tiled=True)

    cot = d_mixed.T
    mine, other = send(cot, TURN), send(cot, TURN_LO)

    gate, up = f32(gate_pre.T), f32(up_pre.T)
    sig = jax.nn.sigmoid(gate)
    act = gate * sig
    hid_own = lax.optimization_barrier(bf16(act * up))
    hid_oth = send(hid_own, PARTNER)

    pair = jnp.where(lo == 0, jnp.stack([mine, other]), jnp.stack([other, mine])).reshape(640, 512)
    pair = first(pair, hid_own)
    cot_a = jnp.zeros((2560, 512), jnp.bfloat16)
    cot_a = lax.dynamic_update_slice(cot_a, pair, (rows(0), zero))
    for d in (1, 3, 2):
        piece = send(pair, ALONG_X[d])
        if d == 2:
            piece, hid_oth = lax.optimization_barrier((piece, hid_oth))
        cot_a = lax.dynamic_update_slice(cot_a, piece, (rows(4 - d), zero))
    cot_b = send(cot_a, SIBLING)

    hid_a = jnp.where(same, hid_own, hid_oth)
    hid_b = jnp.where(same, hid_oth, hid_own)
    hid_a, hid_b = lax.optimization_barrier((hid_a, hid_b))

    grad = dot(cot_a, hid_a, ((1,), (1,))) + dot(cot_b, hid_b, ((1,), (1,)))
    grad = bf16(grad)
    grad_down = f32(
        lax.psum_scatter(grad, "blk", axis_index_groups=PLANES, scatter_dimension=0, tiled=True)
    )
    weight = first(weight, grad[:8, :128])

    part_b = bf16(dot(weight, hid_b, ((1,), (0,))))
    got = send(part_b, SIBLING)
    weight = first(weight, part_b)
    part_a = bf16(dot(weight, hid_a, ((1,), (0,))) + f32(got))
    total = f32(lax.dynamic_slice(part_a, (rows(0), zero), (640, 512)))
    for d in (1, 3, 2):
        piece = lax.dynamic_slice(part_a, (rows(d), zero), (640, 512))
        total = total + f32(send(piece, ALONG_X[d]))
    total = bf16(total)
    keep = lax.dynamic_slice(total, (lo * 320, zero), (320, 512))
    give = lax.dynamic_slice(total, ((1 - lo) * 320, zero), (320, 512))
    mixed = bf16(f32(send(keep, TURN)) + f32(send(give, TURN_LO))).T

    weight = first(weight, part_a)
    dh_a = dot(weight, cot_a, ((0,), (0,)))
    dh_b = dot(weight, cot_b, ((0,), (0,)))
    away = send(bf16(jnp.where(same, dh_b, dh_a)), PARTNER)
    d_hidden = jnp.where(same, dh_a, dh_b) + f32(away)
    d_gate = bf16(d_hidden * up * sig * (1.0 + gate * (1.0 - sig))).T
    d_up = bf16(d_hidden * act).T
    return (mixed, d_gate, d_up, grad_down)


def solution(mesh):
    in_specs = (P("blk", "tp"), P("blk", "tp"), P("blk", "tp"), P("blk", "tp"))
    out_specs = (P("blk", "tp"), P("blk", "tp"), P("blk", "tp"), P("blk", "tp"))
    return jax.shard_map(body, mesh=mesh, in_specs=in_specs, out_specs=out_specs, check_vma=False)
```

```python
import jax
import jax.numpy as jnp
from jax import lax
from jax.sharding import PartitionSpec as P

AXES = ("blk", "tp")
PLANES = [[2 * z + half for z in range(8)] for half in range(2)]


def route(move):
    pairs = []
    for x in range(4):
        for hi in range(2):
            for lo in range(2):
                for z in range(8):
                    for core in range(2):
                        tx, thi, tlo, tz, tcore = move(x, hi, lo, z, core)
                        source = (z * 2 + hi) * 16 + x * 4 + lo * 2 + core
                        target = (tz * 2 + thi) * 16 + (tx % 4) * 4 + tlo * 2 + tcore
                        pairs.append((source, target))
    return pairs


SIBLING = route(lambda x, hi, lo, z, c: (x, hi, lo, z, 1 - c))
PARTNER = route(lambda x, hi, lo, z, c: (x, 1 - hi, lo, z, c))
TURN = route(lambda x, hi, lo, z, c: (x, c, lo, z, hi))
TURN_LO = route(lambda x, hi, lo, z, c: (x, c, 1 - lo, z, hi))
X_FAR = route(lambda x, hi, lo, z, c: (x + 2, hi, lo, z, c))
X_UP = route(lambda x, hi, lo, z, c: (x + 1, hi, lo, z, c))
X_DOWN = route(lambda x, hi, lo, z, c: (x - 1, hi, lo, z, c))


def send(value, pairs):
    return lax.ppermute(value, AXES, pairs)


def f32(value):
    return value.astype(jnp.float32)


def bf16(value):
    return value.astype(jnp.bfloat16)


def dot(left, right, dims):
    return lax.dot_general(left, right, ((dims[0], dims[1]), ((), ())), preferred_element_type=jnp.float32)


def first(value, *after):
    return lax.optimization_barrier((value, *after))[0]


def body(gate_pre, up_pre, down_weight, d_mixed):
    blk, tp = lax.axis_index("blk").astype(jnp.uint32), lax.axis_index("tp").astype(jnp.uint32)
    hi, core, lo, x = blk & 1, tp & 1, (tp >> 1) & 1, tp >> 2
    same = hi == core
    zero = jnp.uint32(0)

    def x_rows(step):
        return ((x + (step & 3)) & 3) * 640

    def put(whole, part, row):
        return lax.dynamic_update_slice(whole, part, (row, zero))

    def rows_of(whole, row, count):
        return lax.dynamic_slice(whole, (row, zero), (count, whole.shape[1]))

    weight = lax.all_gather(down_weight, "blk", axis_index_groups=PLANES, axis=0, tiled=True)

    cot = d_mixed.T
    mine, other = send(cot, TURN), send(cot, TURN_LO)

    gate, up = f32(gate_pre.T), f32(up_pre.T)
    sig = jax.nn.sigmoid(gate)
    act = gate * sig
    hid_own = lax.optimization_barrier(bf16(act * up))
    hid_oth = send(hid_own, PARTNER)

    pair = jnp.where(lo == 0, jnp.stack([mine, other]), jnp.stack([other, mine])).reshape(640, 512)
    pair = first(pair, hid_own)
    left, right = send(pair, X_UP), send(pair, X_DOWN)
    far_l, far_r = send(left[:320], X_UP), send(right[320:], X_DOWN)
    cot_a = put(jnp.zeros((2560, 512), jnp.bfloat16), pair, x_rows(0))
    cot_a = put(cot_a, left, x_rows(-1))
    cot_a = put(cot_a, right, x_rows(1))
    cot_a, far_l, far_r, hid_oth = lax.optimization_barrier((cot_a, far_l, far_r, hid_oth))
    cot_a = put(cot_a, far_l, x_rows(2))
    cot_a = put(cot_a, far_r, x_rows(2) + 320)
    cot_b = send(cot_a, SIBLING)

    hid_a = jnp.where(same, hid_own, hid_oth)
    hid_b = jnp.where(same, hid_oth, hid_own)
    hid_a, hid_b = lax.optimization_barrier((hid_a, hid_b))

    grad = dot(cot_a, hid_a, ((1,), (1,))) + dot(cot_b, hid_b, ((1,), (1,)))
    grad = bf16(grad)
    grad_down = f32(
        lax.psum_scatter(grad, "blk", axis_index_groups=PLANES, scatter_dimension=0, tiled=True)
    )
    weight = first(weight, grad[:8, :128])

    part_b = bf16(dot(weight, hid_b, ((1,), (0,))))
    got = send(part_b, SIBLING)
    weight = first(weight, part_b)
    part_a = bf16(dot(weight, hid_a, ((1,), (0,))) + f32(got))
    total = f32(rows_of(part_a, x_rows(0), 640))
    for d, pairs in ((1, X_UP), (3, X_DOWN), (2, X_FAR)):
        total = total + f32(send(rows_of(part_a, x_rows(d), 640), pairs))
    total = bf16(total)
    keep, give = rows_of(total, lo * 320, 320), rows_of(total, (1 - lo) * 320, 320)
    mixed = bf16(f32(send(keep, TURN)) + f32(send(give, TURN_LO))).T

    weight = first(weight, part_a)
    dh_a = dot(weight, cot_a, ((0,), (0,)))
    dh_b = dot(weight, cot_b, ((0,), (0,)))
    away = send(bf16(jnp.where(same, dh_b, dh_a)), PARTNER)
    d_hidden = jnp.where(same, dh_a, dh_b) + f32(away)
    d_gate = bf16(d_hidden * up * sig * (1.0 + gate * (1.0 - sig))).T
    d_up = bf16(d_hidden * act).T
    return (mixed, d_gate, d_up, grad_down)


def solution(mesh):
    in_specs = (P("blk", "tp"), P("blk", "tp"), P("blk", "tp"), P("blk", "tp"))
    out_specs = (P("blk", "tp"), P("blk", "tp"), P("blk", "tp"), P("blk", "tp"))
    return jax.shard_map(body, mesh=mesh, in_specs=in_specs, out_specs=out_specs, check_vma=False)
```

```python
import jax
import jax.numpy as jnp
from jax import lax
from jax.experimental.layout import Layout, with_layout_constraint
from jax.sharding import PartitionSpec as P

AXES = ("blk", "tp")
PLANES = [[2 * z + half for z in range(8)] for half in range(2)]


def route(move):
    pairs = []
    for x in range(4):
        for hi in range(2):
            for lo in range(2):
                for z in range(8):
                    for core in range(2):
                        tx, thi, tlo, tz, tcore = move(x, hi, lo, z, core)
                        source = (z * 2 + hi) * 16 + x * 4 + lo * 2 + core
                        target = (tz * 2 + thi) * 16 + (tx % 4) * 4 + tlo * 2 + tcore
                        pairs.append((source, target))
    return pairs


SIBLING = route(lambda x, hi, lo, z, c: (x, hi, lo, z, 1 - c))
PARTNER = route(lambda x, hi, lo, z, c: (x, 1 - hi, lo, z, c))
TURN = route(lambda x, hi, lo, z, c: (x, c, lo, z, hi))
TURN_LO = route(lambda x, hi, lo, z, c: (x, c, 1 - lo, z, hi))
X_FAR = route(lambda x, hi, lo, z, c: (x + 2, hi, lo, z, c))
X_UP = route(lambda x, hi, lo, z, c: (x + 1, hi, lo, z, c))
X_DOWN = route(lambda x, hi, lo, z, c: (x - 1, hi, lo, z, c))


def send(value, pairs):
    return lax.ppermute(value, AXES, pairs)


def f32(value):
    return value.astype(jnp.float32)


def bf16(value):
    return value.astype(jnp.bfloat16)


def row_major(value):
    return with_layout_constraint(value, Layout((0, 1)))


def dot(left, right, dims):
    return lax.dot_general(left, right, ((dims[0], dims[1]), ((), ())), preferred_element_type=jnp.float32)


def first(value, *after):
    return lax.optimization_barrier((value, *after))[0]


def body(gate_pre, up_pre, down_weight, d_mixed):
    blk, tp = lax.axis_index("blk").astype(jnp.uint32), lax.axis_index("tp").astype(jnp.uint32)
    hi, core, lo, x = blk & 1, tp & 1, (tp >> 1) & 1, tp >> 2
    same = hi == core
    zero = jnp.uint32(0)

    def x_rows(step):
        return ((x + (step & 3)) & 3) * 640

    def put(whole, part, row):
        return lax.dynamic_update_slice(whole, part, (row, zero))

    def rows_of(whole, row, count):
        return lax.dynamic_slice(whole, (row, zero), (count, whole.shape[1]))

    weight = lax.all_gather(down_weight, "blk", axis_index_groups=PLANES, axis=0, tiled=True)

    cot = d_mixed.T
    mine, other = send(cot, TURN), send(cot, TURN_LO)

    gate, up = f32(gate_pre.T), f32(up_pre.T)
    sig = jax.nn.sigmoid(gate)
    act = gate * sig
    hid_own = lax.optimization_barrier(bf16(act * up))
    hid_oth = send(hid_own, PARTNER)

    pair = jnp.where(lo == 0, jnp.stack([mine, other]), jnp.stack([other, mine])).reshape(640, 512)
    pair = first(pair, hid_own)
    left, right = send(pair, X_UP), send(pair, X_DOWN)
    far_l, far_r = send(left[:320], X_UP), send(right[320:], X_DOWN)
    cot_a = put(jnp.zeros((2560, 512), jnp.bfloat16), pair, x_rows(0))
    cot_a = put(cot_a, left, x_rows(-1))
    cot_a = put(cot_a, right, x_rows(1))
    cot_a, far_l, far_r, hid_oth = lax.optimization_barrier((cot_a, far_l, far_r, hid_oth))
    cot_a = put(cot_a, far_l, x_rows(2))
    cot_a = put(cot_a, far_r, x_rows(2) + 320)
    cot_b = send(cot_a, SIBLING)

    hid_a = jnp.where(same, hid_own, hid_oth)
    hid_b = jnp.where(same, hid_oth, hid_own)
    hid_a, hid_b = lax.optimization_barrier((hid_a, hid_b))

    grad = dot(cot_a, hid_a, ((1,), (1,))) + dot(cot_b, hid_b, ((1,), (1,)))
    grad = bf16(grad)
    grad_down = f32(
        lax.psum_scatter(grad, "blk", axis_index_groups=PLANES, scatter_dimension=0, tiled=True)
    )
    weight = first(weight, grad[:8, :128])

    part_b = row_major(bf16(dot(weight, hid_b, ((1,), (0,)))))
    got = send(part_b, SIBLING)
    weight = first(weight, part_b)
    part_a = row_major(bf16(dot(weight, hid_a, ((1,), (0,))) + f32(got)))
    total = f32(rows_of(part_a, x_rows(0), 640))
    for d, pairs in ((1, X_UP), (3, X_DOWN), (2, X_FAR)):
        total = total + f32(send(rows_of(part_a, x_rows(d), 640), pairs))
    total = bf16(total)
    keep, give = rows_of(total, lo * 320, 320), rows_of(total, (1 - lo) * 320, 320)
    keep, give = send(keep, TURN), send(give, TURN_LO)
    keep, give, grad_down = lax.optimization_barrier((keep, give, grad_down))
    mixed = bf16(f32(keep) + f32(give)).T

    weight = first(weight, part_a)
    dh_a = dot(weight, cot_a, ((0,), (0,)))
    dh_b = dot(weight, cot_b, ((0,), (0,)))
    away = send(bf16(jnp.where(same, dh_b, dh_a)), PARTNER)
    d_hidden = jnp.where(same, dh_a, dh_b) + f32(away)
    d_gate = bf16(d_hidden * up * sig * (1.0 + gate * (1.0 - sig))).T
    d_up = bf16(d_hidden * act).T
    return (mixed, d_gate, d_up, grad_down)


def solution(mesh):
    in_specs = (P("blk", "tp"), P("blk", "tp"), P("blk", "tp"), P("blk", "tp"))
    out_specs = (P("blk", "tp"), P("blk", "tp"), P("blk", "tp"), P("blk", "tp"))
    return jax.shard_map(body, mesh=mesh, in_specs=in_specs, out_specs=out_specs, check_vma=False)
```

```python
import jax
import jax.numpy as jnp
from jax import lax
from jax.experimental.layout import Layout, with_layout_constraint
from jax.sharding import PartitionSpec as P

AXES = ("blk", "tp")
PLANES = [[2 * z + half for z in range(8)] for half in range(2)]


def route(move):
    pairs = []
    for x in range(4):
        for hi in range(2):
            for lo in range(2):
                for z in range(8):
                    for core in range(2):
                        tx, thi, tlo, tz, tcore = move(x, hi, lo, z, core)
                        source = (z * 2 + hi) * 16 + x * 4 + lo * 2 + core
                        target = (tz * 2 + thi) * 16 + (tx % 4) * 4 + tlo * 2 + tcore
                        pairs.append((source, target))
    return pairs


SIBLING = route(lambda x, hi, lo, z, c: (x, hi, lo, z, 1 - c))
PARTNER = route(lambda x, hi, lo, z, c: (x, 1 - hi, lo, z, c))
TURN = route(lambda x, hi, lo, z, c: (x, c, lo, z, hi))
TURN_LO = route(lambda x, hi, lo, z, c: (x, c, 1 - lo, z, hi))
X_FAR = route(lambda x, hi, lo, z, c: (x + 2, hi, lo, z, c))
X_UP = route(lambda x, hi, lo, z, c: (x + 1, hi, lo, z, c))
X_DOWN = route(lambda x, hi, lo, z, c: (x - 1, hi, lo, z, c))


def send(value, pairs):
    return lax.ppermute(value, AXES, pairs)


def f32(value):
    return value.astype(jnp.float32)


def bf16(value):
    return value.astype(jnp.bfloat16)


def row_major(value):
    return with_layout_constraint(value, Layout((0, 1)))


def dot(left, right, dims):
    return lax.dot_general(left, right, ((dims[0], dims[1]), ((), ())), preferred_element_type=jnp.float32)


def first(value, *after):
    return lax.optimization_barrier((value, *after))[0]


def body(gate_pre, up_pre, down_weight, d_mixed):
    blk, tp = lax.axis_index("blk").astype(jnp.uint32), lax.axis_index("tp").astype(jnp.uint32)
    hi, core, lo, x = blk & 1, tp & 1, (tp >> 1) & 1, tp >> 2
    same = hi == core
    zero = jnp.uint32(0)

    def x_rows(step):
        return ((x + (step & 3)) & 3) * 640

    def put(whole, part, row):
        return lax.dynamic_update_slice(whole, part, (row, zero))

    def rows_of(whole, row, count):
        return lax.dynamic_slice(whole, (row, zero), (count, whole.shape[1]))

    weight = lax.all_gather(down_weight, "blk", axis_index_groups=PLANES, axis=0, tiled=True)

    cot = d_mixed.T
    mine, other = send(cot, TURN), send(cot, TURN_LO)

    gate, up = f32(gate_pre.T), f32(up_pre.T)
    sig = jax.nn.sigmoid(gate)
    act = gate * sig
    hid_own = lax.optimization_barrier(bf16(act * up))
    hid_oth = send(hid_own, PARTNER)

    pair = jnp.where(lo == 0, jnp.stack([mine, other]), jnp.stack([other, mine])).reshape(640, 512)
    pair = first(pair, hid_own)
    left, right = send(pair, X_UP), send(pair, X_DOWN)
    far_l, far_r = send(left[:320], X_UP), send(right[320:], X_DOWN)
    cot_a = put(jnp.zeros((2560, 512), jnp.bfloat16), pair, x_rows(0))
    cot_a = put(cot_a, left, x_rows(-1))
    cot_a = put(cot_a, right, x_rows(1))
    cot_a, far_l, far_r, hid_oth = lax.optimization_barrier((cot_a, far_l, far_r, hid_oth))
    cot_a = put(cot_a, far_l, x_rows(2))
    cot_a = put(cot_a, far_r, x_rows(2) + 320)
    cot_b = send(cot_a, SIBLING)

    hid_a = jnp.where(same, hid_own, hid_oth)
    hid_b = jnp.where(same, hid_oth, hid_own)
    hid_a, hid_b = lax.optimization_barrier((hid_a, hid_b))

    grad = dot(cot_a, hid_a, ((1,), (1,))) + dot(cot_b, hid_b, ((1,), (1,)))
    grad = bf16(grad)
    grad_down = f32(
        lax.psum_scatter(grad, "blk", axis_index_groups=PLANES, scatter_dimension=0, tiled=True)
    )
    cot_keep, cot_away = jnp.where(same, cot_a, cot_b), jnp.where(same, cot_b, cot_a)
    cot_keep, cot_away = lax.optimization_barrier((cot_keep, cot_away, grad[:8, :128]))[:2]
    weight = first(weight, cot_keep, cot_away)

    part_b = row_major(bf16(dot(weight, hid_b, ((1,), (0,)))))
    got = send(part_b, SIBLING)
    weight = first(weight, part_b)
    part_a = row_major(bf16(dot(weight, hid_a, ((1,), (0,))) + f32(got)))
    def cut(step, row):
        return rows_of(part_a, x_rows(step) + row, 320)

    slices = (cut(2, 0), cut(2, 320), cut(1, 320), cut(3, 0), cut(1, 0), cut(3, 320))
    far_l, far_r, plain_l, plain_r, joint_l, joint_r = lax.optimization_barrier(slices)
    weight = first(weight, far_l, far_r, plain_l, plain_r, joint_l, joint_r)
    far_l, far_r = send(far_l, X_UP), send(far_r, X_DOWN)
    plain_l, plain_r = send(plain_l, X_UP), send(plain_r, X_DOWN)

    away = bf16(dot(weight, cot_away, ((0,), (0,))))
    far_l, far_r, away = lax.optimization_barrier((far_l, far_r, away))
    joint_l, joint_r = bf16(f32(joint_l) + f32(far_l)), bf16(f32(joint_r) + f32(far_r))
    joint_l, joint_r, weight = lax.optimization_barrier((joint_l, joint_r, weight))
    keep_dh = dot(weight, cot_keep, ((0,), (0,)))
    joint_l, joint_r = send(joint_l, X_UP), send(joint_r, X_DOWN)
    joint_l, joint_r, plain_l, plain_r, keep_dh = lax.optimization_barrier((joint_l, joint_r, plain_l, plain_r, keep_dh))

    def block(lower):
        left, right = jnp.where(lower, joint_l, plain_l), jnp.where(lower, plain_r, joint_r)
        return bf16(f32(cut(0, jnp.where(lower, zero, jnp.uint32(320)))) + f32(left) + f32(right))

    keep, give = block(lo == 0), block(lo == 1)
    keep, give = send(keep, TURN), send(give, TURN_LO)
    mixed = bf16(f32(keep) + f32(give)).T

    d_hidden = keep_dh + f32(send(away, PARTNER))
    d_gate = bf16(d_hidden * up * sig * (1.0 + gate * (1.0 - sig))).T
    d_up = bf16(d_hidden * act).T
    return (mixed, d_gate, d_up, grad_down)


def solution(mesh):
    in_specs = (P("blk", "tp"), P("blk", "tp"), P("blk", "tp"), P("blk", "tp"))
    out_specs = (P("blk", "tp"), P("blk", "tp"), P("blk", "tp"), P("blk", "tp"))
    return jax.shard_map(body, mesh=mesh, in_specs=in_specs, out_specs=out_specs, check_vma=False)
```

```python
import jax
import jax.numpy as jnp
from jax import lax
from jax.experimental.layout import Layout, with_layout_constraint
from jax.sharding import PartitionSpec as P

AXES = ("blk", "tp")
PLANES = [[2 * z + half for z in range(8)] for half in range(2)]


def route(move):
    pairs = []
    for x in range(4):
        for hi in range(2):
            for lo in range(2):
                for z in range(8):
                    for core in range(2):
                        tx, thi, tlo, tz, tcore = move(x, hi, lo, z, core)
                        source = (z * 2 + hi) * 16 + x * 4 + lo * 2 + core
                        target = (tz * 2 + thi) * 16 + (tx % 4) * 4 + tlo * 2 + tcore
                        pairs.append((source, target))
    return pairs


SIBLING = route(lambda x, hi, lo, z, c: (x, hi, lo, z, 1 - c))
PARTNER = route(lambda x, hi, lo, z, c: (x, 1 - hi, lo, z, c))
TURN = route(lambda x, hi, lo, z, c: (x, c, lo, z, hi))
TURN_LO = route(lambda x, hi, lo, z, c: (x, c, 1 - lo, z, hi))
X_FAR = route(lambda x, hi, lo, z, c: (x + 2, hi, lo, z, c))
X_UP = route(lambda x, hi, lo, z, c: (x + 1, hi, lo, z, c))
X_DOWN = route(lambda x, hi, lo, z, c: (x - 1, hi, lo, z, c))


def send(value, pairs):
    return lax.ppermute(value, AXES, pairs)


def f32(value):
    return value.astype(jnp.float32)


def bf16(value):
    return value.astype(jnp.bfloat16)


def row_major(value):
    return with_layout_constraint(value, Layout((0, 1)))


def dot(left, right, dims):
    return lax.dot_general(left, right, ((dims[0], dims[1]), ((), ())), preferred_element_type=jnp.float32)


def first(value, *after):
    return lax.optimization_barrier((value, *after))[0]


def body(gate_pre, up_pre, down_weight, d_mixed):
    blk, tp = lax.axis_index("blk").astype(jnp.uint32), lax.axis_index("tp").astype(jnp.uint32)
    hi, core, lo, x = blk & 1, tp & 1, (tp >> 1) & 1, tp >> 2
    same = hi == core
    zero = jnp.uint32(0)

    def x_rows(step):
        return ((x + (step & 3)) & 3) * 640

    def put(whole, part, row):
        return lax.dynamic_update_slice(whole, part, (row, zero))

    def rows_of(whole, row, count):
        return lax.dynamic_slice(whole, (row, zero), (count, whole.shape[1]))

    weight = lax.all_gather(down_weight, "blk", axis_index_groups=PLANES, axis=0, tiled=True)

    cot = d_mixed.T
    mine, other = send(cot, TURN), send(cot, TURN_LO)

    gate, up = f32(gate_pre.T), f32(up_pre.T)
    sig = jax.nn.sigmoid(gate)
    act = gate * sig
    hid_own = lax.optimization_barrier(bf16(act * up))
    hid_oth = send(hid_own, PARTNER)

    pair = jnp.where(lo == 0, jnp.stack([mine, other]), jnp.stack([other, mine])).reshape(640, 512)
    pair = first(pair, hid_own)
    left, right = send(pair, X_UP), send(pair, X_DOWN)
    far_l, far_r = send(left[:320], X_UP), send(right[320:], X_DOWN)
    cot_a = put(jnp.zeros((2560, 512), jnp.bfloat16), pair, x_rows(0))
    cot_a = put(cot_a, left, x_rows(-1))
    cot_a = put(cot_a, right, x_rows(1))
    cot_a, far_l, far_r, hid_oth = lax.optimization_barrier((cot_a, far_l, far_r, hid_oth))
    cot_a = put(cot_a, far_l, x_rows(2))
    cot_a = put(cot_a, far_r, x_rows(2) + 320)
    cot_b = send(cot_a, SIBLING)

    hid_a = jnp.where(same, hid_own, hid_oth)
    hid_b = jnp.where(same, hid_oth, hid_own)
    hid_a, hid_b = lax.optimization_barrier((hid_a, hid_b))

    grad = dot(cot_a, hid_a, ((1,), (1,))) + dot(cot_b, hid_b, ((1,), (1,)))
    grad = bf16(grad)
    grad_down = f32(
        lax.psum_scatter(grad, "blk", axis_index_groups=PLANES, scatter_dimension=0, tiled=True)
    )
    cot_keep, cot_away = jnp.where(same, cot_a, cot_b), jnp.where(same, cot_b, cot_a)
    cot_keep, cot_away = lax.optimization_barrier((cot_keep, cot_away, grad[:8, :128]))[:2]
    weight = first(weight, cot_keep, cot_away)

    part_b = row_major(bf16(dot(weight, hid_b, ((1,), (0,)))))
    got = send(part_b, SIBLING)
    weight = first(weight, part_b)
    part_a = row_major(bf16(dot(weight, hid_a, ((1,), (0,))) + f32(got)))
    def cut(step, row):
        return rows_of(part_a, x_rows(step) + row, 320)

    slices = (cut(2, 0), cut(2, 320), cut(1, 320), cut(3, 0), cut(1, 0), cut(3, 320))
    far_l, far_r, plain_l, plain_r, joint_l, joint_r = lax.optimization_barrier(slices)
    weight = first(weight, far_l, far_r, plain_l, plain_r, joint_l, joint_r)
    far_l, far_r = send(far_l, X_UP), send(far_r, X_DOWN)
    plain_l, plain_r = send(plain_l, X_UP), send(plain_r, X_DOWN)

    away = bf16(dot(weight, cot_away, ((0,), (0,))))
    far_l, far_r, away = lax.optimization_barrier((far_l, far_r, away))
    joint_l, joint_r = bf16(f32(joint_l) + f32(far_l)), bf16(f32(joint_r) + f32(far_r))
    joint_l, joint_r, weight = lax.optimization_barrier((joint_l, joint_r, weight))
    keep_dh = dot(weight, cot_keep, ((0,), (0,)))
    joint_l, joint_r = send(joint_l, X_UP), send(joint_r, X_DOWN)
    joint_l, joint_r, plain_l, plain_r, keep_dh = lax.optimization_barrier((joint_l, joint_r, plain_l, plain_r, keep_dh))

    def block(lower):
        left, right = jnp.where(lower, joint_l, plain_l), jnp.where(lower, plain_r, joint_r)
        return bf16(f32(cut(0, jnp.where(lower, zero, jnp.uint32(320)))) + f32(left) + f32(right))

    keep, give = block(lo == 0), block(lo == 1)
    keep, give = send(keep, TURN), send(give, TURN_LO)
    keep, give, grad_down = lax.optimization_barrier((keep, give, grad_down))
    mixed = bf16(f32(keep) + f32(give)).T

    d_hidden = keep_dh + f32(send(away, PARTNER))
    d_gate = bf16(d_hidden * up * sig * (1.0 + gate * (1.0 - sig))).T
    d_up = bf16(d_hidden * act).T
    return (mixed, d_gate, d_up, grad_down)


def solution(mesh):
    in_specs = (P("blk", "tp"), P("blk", "tp"), P("blk", "tp"), P("blk", "tp"))
    out_specs = (P("blk", "tp"), P("blk", "tp"), P("blk", "tp"), P("blk", "tp"))
    return jax.shard_map(body, mesh=mesh, in_specs=in_specs, out_specs=out_specs, check_vma=False)
```

```python
import jax
import jax.numpy as jnp
from jax import lax
from jax.experimental.layout import Layout, with_layout_constraint
from jax.sharding import PartitionSpec as P

AXES = ("blk", "tp")
PLANES = [[2 * z + half for z in range(8)] for half in range(2)]


def route(move):
    pairs = []
    for x in range(4):
        for hi in range(2):
            for lo in range(2):
                for z in range(8):
                    for core in range(2):
                        tx, thi, tlo, tz, tcore = move(x, hi, lo, z, core)
                        source = (z * 2 + hi) * 16 + x * 4 + lo * 2 + core
                        target = (tz * 2 + thi) * 16 + (tx % 4) * 4 + tlo * 2 + tcore
                        pairs.append((source, target))
    return pairs


SIBLING = route(lambda x, hi, lo, z, c: (x, hi, lo, z, 1 - c))
PARTNER = route(lambda x, hi, lo, z, c: (x, 1 - hi, lo, z, c))
TURN = route(lambda x, hi, lo, z, c: (x, c, lo, z, hi))
TURN_LO = route(lambda x, hi, lo, z, c: (x, c, 1 - lo, z, hi))
X_FAR = route(lambda x, hi, lo, z, c: (x + 2, hi, lo, z, c))
X_UP = route(lambda x, hi, lo, z, c: (x + 1, hi, lo, z, c))
X_DOWN = route(lambda x, hi, lo, z, c: (x - 1, hi, lo, z, c))


def send(value, pairs):
    return lax.ppermute(value, AXES, pairs)


def f32(value):
    return value.astype(jnp.float32)


def bf16(value):
    return value.astype(jnp.bfloat16)


def row_major(value):
    return with_layout_constraint(value, Layout((0, 1)))


def dot(left, right, dims):
    return lax.dot_general(left, right, ((dims[0], dims[1]), ((), ())), preferred_element_type=jnp.float32)


def first(value, *after):
    return lax.optimization_barrier((value, *after))[0]


def body(gate_pre, up_pre, down_weight, d_mixed):
    blk, tp = lax.axis_index("blk").astype(jnp.uint32), lax.axis_index("tp").astype(jnp.uint32)
    hi, core, lo, x = blk & 1, tp & 1, (tp >> 1) & 1, tp >> 2
    same = hi == core
    zero = jnp.uint32(0)

    def x_rows(step):
        return ((x + (step & 3)) & 3) * 640

    def put(whole, part, row):
        return lax.dynamic_update_slice(whole, part, (row, zero))

    def rows_of(whole, row, count):
        return lax.dynamic_slice(whole, (row, zero), (count, whole.shape[1]))

    weight = lax.all_gather(down_weight, "blk", axis_index_groups=PLANES, axis=0, tiled=True)

    cot = d_mixed.T
    mine, other = send(cot, TURN), send(cot, TURN_LO)

    gate, up = f32(gate_pre.T), f32(up_pre.T)
    sig = jax.nn.sigmoid(gate)
    act = gate * sig
    hid_own = lax.optimization_barrier(bf16(act * up))
    hid_oth = send(hid_own, PARTNER)

    pair = jnp.where(lo == 0, jnp.stack([mine, other]), jnp.stack([other, mine])).reshape(640, 512)
    pair = first(pair, hid_own)
    left, right = send(pair, X_UP), send(pair, X_DOWN)
    far_l, far_r = send(left[:320], X_UP), send(right[320:], X_DOWN)
    cot_a = put(jnp.zeros((2560, 512), jnp.bfloat16), pair, x_rows(0))
    cot_a = put(cot_a, left, x_rows(-1))
    cot_a = put(cot_a, right, x_rows(1))
    cot_a, far_l, far_r, hid_oth = lax.optimization_barrier((cot_a, far_l, far_r, hid_oth))
    cot_a = put(cot_a, far_l, x_rows(2))
    cot_a = put(cot_a, far_r, x_rows(2) + 320)
    cot_b = send(cot_a, SIBLING)

    hid_a = jnp.where(same, hid_own, hid_oth)
    hid_b = jnp.where(same, hid_oth, hid_own)
    hid_a, hid_b = lax.optimization_barrier((hid_a, hid_b))

    grad = dot(cot_a, hid_a, ((1,), (1,))) + dot(cot_b, hid_b, ((1,), (1,)))
    grad = bf16(grad)
    grad_down = f32(
        lax.psum_scatter(grad, "blk", axis_index_groups=PLANES, scatter_dimension=0, tiled=True)
    )
    cot_keep, cot_away = jnp.where(same, cot_a, cot_b), jnp.where(same, cot_b, cot_a)
    weight = first(weight, grad[:8, :128])

    part_b = row_major(bf16(dot(weight, hid_b, ((1,), (0,)))))
    got = send(part_b, SIBLING)
    weight = first(weight, part_b)
    part_a = row_major(bf16(dot(weight, hid_a, ((1,), (0,))) + f32(got)))
    def cut(step, row):
        return rows_of(part_a, x_rows(step) + row, 320)

    slices = (cut(2, 0), cut(2, 320), cut(1, 320), cut(3, 0), cut(1, 0), cut(3, 320))
    far_l, far_r, plain_l, plain_r, joint_l, joint_r = lax.optimization_barrier(slices)
    weight = first(weight, far_l, far_r, plain_l, plain_r, joint_l, joint_r)
    far_l, far_r = send(far_l, X_UP), send(far_r, X_DOWN)
    plain_l, plain_r = send(plain_l, X_UP), send(plain_r, X_DOWN)

    away = bf16(dot(weight, cot_away, ((0,), (0,))))
    far_l, far_r, away = lax.optimization_barrier((far_l, far_r, away))
    joint_l, joint_r = bf16(f32(joint_l) + f32(far_l)), bf16(f32(joint_r) + f32(far_r))
    joint_l, joint_r, weight = lax.optimization_barrier((joint_l, joint_r, weight))
    keep_dh = dot(weight, cot_keep, ((0,), (0,)))
    joint_l, joint_r = send(joint_l, X_UP), send(joint_r, X_DOWN)
    joint_l, joint_r, plain_l, plain_r, keep_dh = lax.optimization_barrier((joint_l, joint_r, plain_l, plain_r, keep_dh))

    def block(lower):
        left, right = jnp.where(lower, joint_l, plain_l), jnp.where(lower, plain_r, joint_r)
        return bf16(f32(cut(0, jnp.where(lower, zero, jnp.uint32(320)))) + f32(left) + f32(right))

    keep, give = block(lo == 0), block(lo == 1)
    keep, give = send(keep, TURN), send(give, TURN_LO)
    keep, give, grad_down = lax.optimization_barrier((keep, give, grad_down))
    mixed = bf16(f32(keep) + f32(give)).T

    d_hidden = keep_dh + f32(send(away, PARTNER))
    d_gate = bf16(d_hidden * up * sig * (1.0 + gate * (1.0 - sig))).T
    d_up = bf16(d_hidden * act).T
    return (mixed, d_gate, d_up, grad_down)


def solution(mesh):
    in_specs = (P("blk", "tp"), P("blk", "tp"), P("blk", "tp"), P("blk", "tp"))
    out_specs = (P("blk", "tp"), P("blk", "tp"), P("blk", "tp"), P("blk", "tp"))
    return jax.shard_map(body, mesh=mesh, in_specs=in_specs, out_specs=out_specs, check_vma=False)
```
